32 devices in a mesh: loop: 8 (over z, core), rep: 4 (over y, x).
Axes of the slice: x: 2, y: 2, z: 4, core: 2. Of those that a mesh axis runs over, the one named last changes fastest.
Arguments:
- lam: bfloat16 [8, 384, 1024], P(None, None, ('rep', 'loop')), may hold values from -6 to 6
- integrals: bfloat16 [8, 1024, 2048], P(None, 'rep', 'loop'), may hold values from -0.1875 to 0.1875
- block_mask: int32 [8, 32], P(None, 'rep'), may hold values 0 or 1
Outputs:
- ladder: bfloat16 [8, 384, 2048], P(None, 'rep', 'loop')
The draws below stay inside these ranges and needn't reach their ends.
All inputs are finite; a program needn't handle non-finite values. No bound on the sum of `block_mask` on one device may be relied on, other than what follows from the above.
Results may differ from the reference program's by a relative error of at most 0.001.
Values may be sent and summed in bfloat16 or wider, within the bound.
No kernel may reach another device: no remote copies, remote signals or barrier semaphores. Data moves between devices by JAX's collectives and lax.ppermute only.
A program may use at most 64 MiB of HBM per device.

```python
import jax
import jax.numpy as jnp
from jax import lax

NIRREP = 8
OCC_PAIRS = 384
CBH = 32
CDBLOCKS = 32
CDH = 1024
ABH = 2048


def place_ends(drawn, rng, least, top_value):
    longest = drawn.shape.index(max(drawn.shape))
    spots = []
    for shift in (0, 1):
        where = [jax.random.randint(jax.random.fold_in(rng, axis), (), 0, length) for axis, length in enumerate(drawn.shape)]
        where[longest] = (where[longest] + shift) % drawn.shape[longest]
        spots.append(tuple(where))
    return drawn.at[spots[0]].set(least).at[spots[1]].set(top_value)


def steps_of(key, extent, pieces, low, top_value):
    loudness = 1.0
    for axis_at, shards_of in pieces:
        draws = jax.random.uniform(jax.random.fold_in(jax.random.fold_in(key, 6), axis_at), (shards_of,), jnp.float32, low / len(pieces), top_value / len(pieces))
        loudness = loudness * jnp.repeat(jnp.exp(draws), extent[axis_at] // shards_of).reshape((-1,) + (1,) * (len(extent) - 1 - axis_at))
    return loudness


def bell_draw(rng, dims, width, most, shards=(), held_as=jnp.bfloat16):
    result = width * jax.random.normal(rng, dims, jnp.float32)
    if shards:
        result = result * steps_of(rng, dims, shards, -0.22, 0.18)
    return jnp.clip(result, -most, most).astype(held_as)


def setup_inputs(seed: int = 0) -> dict:
    arg_keys = jax.random.split(jax.random.key(seed), 4)
    lam = bell_draw(arg_keys[0], (NIRREP, OCC_PAIRS, CDH), 1.0, 6.0, ((2, 32),))
    integrals = bell_draw(arg_keys[1], (NIRREP, CDH, ABH), CDH ** -0.5, 0.1875, ((1, 4), (2, 8)))
    block_mask = place_ends((jax.random.randint(arg_keys[2], (NIRREP, CDBLOCKS), 0, 8) < 7).astype(jnp.int32), jax.random.fold_in(arg_keys[2], 1), 0, 1)
    return dict(lam=lam, integrals=integrals, block_mask=block_mask)


def reference(lam, integrals, block_mask):
    def one_irrep(index):
        amplitudes = lam[index]
        weights = integrals[index]
        live = jnp.repeat(block_mask[index], CBH) == 1
        kept = jnp.where(live[:, None], weights, jnp.zeros_like(weights))
        return jnp.dot(amplitudes, kept, preferred_element_type=jnp.float32).astype(jnp.bfloat16)

    return lax.map(one_irrep, jnp.arange(NIRREP, dtype=jnp.int32))
```

```python
import functools

import jax
import jax.numpy as jnp
from jax import lax
from jax.experimental import pallas as pl
from jax.experimental.pallas import tpu as pltpu
from jax.sharding import PartitionSpec as P

VMEM = pltpu.VMEM


def pack_kernel(halves, mask_ref, lam_ref, own_ref, to_x_ref, to_y_ref, turned):
    spot = lax.axis_index("loop")
    y, x = lax.axis_index("rep") // 2, lax.axis_index("rep") % 2
    rows = turned.shape[2]
    for kind in range(2):
        live = [mask_ref[kind * halves + h, spot] == 1 for h in range(halves)]
        block = jnp.concatenate(
            [jnp.where(live[h], lam_ref[kind * halves + h], 0).astype(jnp.bfloat16) for h in range(halves)], axis=0
        )
        flipped = block.T
        for quarter in range(4):
            turned[kind, quarter] = flipped[quarter * rows : (quarter + 1) * rows]
    ny, nx = 1 - y, 1 - x
    own_ref[0, 0] = turned[0, ny * 2 + x]
    own_ref[0, 1] = turned[1, y * 2 + nx]
    own_ref[1, 0] = turned[0, y * 2 + x]
    own_ref[1, 1] = turned[1, y * 2 + x]
    to_x_ref[0] = turned[0, ny * 2 + nx]
    to_x_ref[1] = turned[0, y * 2 + nx]
    to_y_ref[0] = turned[1, ny * 2 + nx]
    to_y_ref[1] = turned[1, ny * 2 + x]


def products(mine_ref, other_ref, own_ref, from_x_ref, from_y_ref, pieces):
    spot = lax.axis_index("loop")
    chips = mine_ref.shape[0]
    z, core = spot // 2, spot % 2
    for step in range(chips):
        source = lax.rem(z - step + chips, chips) * 2
        pieces[source + core] = mine_ref[step]
        pieces[source + 1 - core] = other_ref[step]
    halves = from_x_ref.shape[0]
    depth = pieces.shape[3] // halves
    for kind, far_ref in ((0, from_x_ref), (1, from_y_ref)):
        near = [pieces[s, kind] for s in range(2 * chips)]
        far = [pieces[s, 2 + kind] for s in range(2 * chips)]
        for h in range(halves):
            cut = slice(h * depth, (h + 1) * depth)
            near_lam = jnp.concatenate([p[:, cut] for p in near], axis=1)
            far_lam = jnp.concatenate([p[:, cut] for p in far], axis=1)
            yield kind * halves + h, (
                jnp.dot(near_lam, own_ref[kind * halves + h], preferred_element_type=jnp.float32)
                + jnp.dot(far_lam, far_ref[h], preferred_element_type=jnp.float32)
            )


def sent_kernel(mine_ref, other_ref, own_ref, from_x_ref, from_y_ref, to_y_ref, to_x_ref, pieces):
    halves = from_x_ref.shape[0]
    for h, value in products(mine_ref, other_ref, own_ref, from_x_ref, from_y_ref, pieces):
        if h < halves:
            to_y_ref[h] = value
        else:
            to_x_ref[h - halves] = value


def kept_kernel(mine_ref, other_ref, own_ref, from_x_ref, from_y_ref, sum_y_ref, sum_x_ref, out_ref, pieces):
    halves = from_x_ref.shape[0]
    for h, value in products(mine_ref, other_ref, own_ref, from_x_ref, from_y_ref, pieces):
        arrived = sum_y_ref[h] if h < halves else sum_x_ref[h - halves]
        out_ref[h] = (value + arrived).astype(out_ref.dtype)


def square(lam, integrals, block_mask):
    irreps, occ, depth = lam.shape
    halves = irreps // 2
    rows = occ // 4
    columns = integrals.shape[2]
    loops = lax.axis_size("loop")
    chips = loops // 2
    over_x = [(r, r ^ 1) for r in range(4)]
    over_y = [(r, r ^ 2) for r in range(4)]
    over_core = [(s, s ^ 1) for s in range(loops)]
    turn = lambda k: [(s, (s + 2 * k) % loops) for s in range(loops)]
    bf16, f32 = jnp.bfloat16, jnp.float32
    lanes = halves * depth

    own, to_x, to_y = pl.pallas_call(
        functools.partial(pack_kernel, halves),
        out_shape=(
            jax.ShapeDtypeStruct((2, 2, rows, lanes), bf16),
            jax.ShapeDtypeStruct((2, rows, lanes), bf16),
            jax.ShapeDtypeStruct((2, rows, lanes), bf16),
        ),
        in_specs=[pl.BlockSpec(memory_space=pltpu.SMEM), pl.BlockSpec(memory_space=VMEM)],
        out_specs=[pl.BlockSpec(memory_space=VMEM)] * 3,
        scratch_shapes=[VMEM((2, 4, rows, lanes), bf16)],
    )(block_mask, lam.transpose(0, 2, 1))

    lam_x = lax.ppermute(to_x, "rep", over_x)
    lam_y = lax.ppermute(to_y, "rep", over_y)
    far_x = lax.ppermute(integrals[:halves], "rep", over_x)
    far_y = lax.ppermute(integrals[halves:], "rep", over_y)

    def gathered(which):
        mine = jnp.concatenate([own[which], lam_x[which][None], lam_y[which][None]], axis=0)
        mine = jnp.stack([mine] + [lax.ppermute(mine, "loop", turn(k)) for k in range(1, chips)])
        return mine, lax.ppermute(mine, "loop", over_core)

    scratch = [VMEM((loops, 4, rows, lanes), bf16)]
    mine, other = gathered(0)
    partial_y, partial_x = pl.pallas_call(
        sent_kernel,
        out_shape=(jax.ShapeDtypeStruct((halves, rows, columns), f32),) * 2,
        in_specs=[pl.BlockSpec(memory_space=VMEM)] * 5,
        out_specs=[pl.BlockSpec(memory_space=VMEM)] * 2,
        scratch_shapes=scratch,
    )(mine, other, integrals, far_x, far_y)
    sum_y = lax.ppermute(partial_y, "rep", over_y)
    sum_x = lax.ppermute(partial_x, "rep", over_x)
    mine, other = gathered(1)
    return pl.pallas_call(
        kept_kernel,
        out_shape=jax.ShapeDtypeStruct((irreps, rows, columns), bf16),
        in_specs=[pl.BlockSpec(memory_space=VMEM)] * 7,
        out_specs=pl.BlockSpec(memory_space=VMEM),
        scratch_shapes=scratch,
    )(mine, other, integrals, far_x, far_y, sum_y, sum_x)


def general(lam, integrals, block_mask):
    live = jnp.repeat(block_mask, lam.shape[2], axis=1) == 1
    kept = jnp.where(live[:, :, None], integrals, jnp.zeros_like(integrals))
    layer_lam = lax.all_gather(lam, "loop", axis=2, tiled=True)
    partial_sum = jnp.einsum("hpk,hka->hpa", layer_lam, kept, preferred_element_type=jnp.float32)
    return lax.psum_scatter(partial_sum, "rep", scatter_dimension=1, tiled=True).astype(jnp.bfloat16)


def solution(mesh):
    return jax.shard_map(
        square if mesh.shape["rep"] == 4 else general,
        mesh=mesh,
        in_specs=(P(None, None, ("rep", "loop")), P(None, "rep", "loop"), P(None, "rep")),
        out_specs=P(None, "rep", "loop"),
        check_vma=False,
    )
```

```python
import functools

import jax
import jax.numpy as jnp
from jax import lax
from jax.experimental import pallas as pl
from jax.experimental.pallas import tpu as pltpu
from jax.sharding import PartitionSpec as P

VMEM = pltpu.VMEM
PARAMS = pltpu.CompilerParams(vmem_limit_bytes=16 << 20)
CHIPS = 4


def pack_kernel(halves, lam_ref, own_ref, to_x_ref, to_y_ref, turned):
    y, x = lax.axis_index("rep") // 2, lax.axis_index("rep") % 2
    rows = turned.shape[2]
    for kind in range(2):
        block = jnp.concatenate([lam_ref[kind * halves + h] for h in range(halves)], axis=0)
        flipped = block.T
        for quarter in range(4):
            turned[kind, quarter] = flipped[quarter * rows : (quarter + 1) * rows]
    ny, nx = 1 - y, 1 - x
    own_ref[0, 0] = turned[0, ny * 2 + x]
    own_ref[0, 1] = turned[1, y * 2 + nx]
    own_ref[1, 0] = turned[0, y * 2 + x]
    own_ref[1, 1] = turned[1, y * 2 + x]
    to_x_ref[0] = turned[0, ny * 2 + nx]
    to_x_ref[1] = turned[0, y * 2 + nx]
    to_y_ref[0] = turned[1, ny * 2 + nx]
    to_y_ref[1] = turned[1, ny * 2 + x]


def product_kernel(
    mine_ref, sibling_ref, one_ref, two_ref, three_ref, three_sibling_ref,
    near_x_ref, near_y_ref, from_x_ref, from_y_ref, first_ref, last_ref, pieces,
):
    spot = lax.axis_index("loop")
    z, core = spot // 2, spot % 2

    def block(back, of_core):
        return lax.rem(z - back + CHIPS, CHIPS) * 2 + of_core

    pieces[block(0, core)] = mine_ref[...]
    pieces[block(0, 1 - core)] = sibling_ref[...]
    pieces[block(3, core)] = three_ref[...]
    pieces[block(3, 1 - core)] = three_sibling_ref[...]
    held, other = 1 + core, 2 - core
    pieces[block(held, core)] = one_ref[0]
    pieces[block(held, 1 - core)] = one_ref[1]
    pieces[block(other, 1 - core)] = two_ref[0]
    pieces[block(other, core)] = two_ref[1]
    halves = from_x_ref.shape[0]
    depth = pieces.shape[3] // halves
    for kind, near_ref, far_ref, out_ref in ((0, near_x_ref, from_x_ref, first_ref), (1, near_y_ref, from_y_ref, last_ref)):
        near = [pieces[s, kind] for s in range(2 * CHIPS)]
        far = [pieces[s, 2 + kind] for s in range(2 * CHIPS)]
        for h in range(halves):
            cut = slice(h * depth, (h + 1) * depth)
            near_lam = jnp.concatenate([p[:, cut] for p in near], axis=1)
            far_lam = jnp.concatenate([p[:, cut] for p in far], axis=1)
            out_ref[h] = jnp.dot(near_lam, near_ref[h], preferred_element_type=jnp.float32) + jnp.dot(
                far_lam, far_ref[h], preferred_element_type=jnp.float32
            )


def total_kernel(first_ref, last_ref, sum_y_ref, sum_x_ref, out_ref):
    halves = first_ref.shape[0]
    out_ref[:halves] = (first_ref[...] + sum_y_ref[...]).astype(out_ref.dtype)
    out_ref[halves:] = (last_ref[...] + sum_x_ref[...]).astype(out_ref.dtype)


def square(lam, integrals, block_mask):
    irreps, occ, depth = lam.shape
    halves = irreps // 2
    rows = occ // 4
    columns = integrals.shape[2]
    loops = 2 * CHIPS
    over_x = [(r, r ^ 1) for r in range(4)]
    over_y = [(r, r ^ 2) for r in range(4)]
    over_core = [(s, s ^ 1) for s in range(loops)]
    by_three = [(s, (s + 6) % loops) for s in range(loops)]
    by_core = [(s, (s + 2 + 2 * (s % 2)) % loops) for s in range(loops)]
    bf16, f32 = jnp.bfloat16, jnp.float32
    lanes = halves * depth
    sums = jax.ShapeDtypeStruct((halves, rows, columns), f32)
    in_vmem = pl.BlockSpec(memory_space=VMEM)

    live = lax.dynamic_slice_in_dim(block_mask, lax.axis_index("loop"), 1, 1)[:, :, None] == 1
    masked = jnp.where(live, lam.transpose(0, 2, 1), jnp.zeros((), bf16))
    own, to_x, to_y = pl.pallas_call(
        functools.partial(pack_kernel, halves),
        out_shape=(
            jax.ShapeDtypeStruct((2, 2, rows, lanes), bf16),
            jax.ShapeDtypeStruct((2, rows, lanes), bf16),
            jax.ShapeDtypeStruct((2, rows, lanes), bf16),
        ),
        in_specs=[in_vmem],
        out_specs=[in_vmem] * 3,
        scratch_shapes=[VMEM((2, 4, rows, lanes), bf16)],
        compiler_params=PARAMS,
    )(masked)

    lam_x = lax.ppermute(to_x, "rep", over_x)
    lam_y = lax.ppermute(to_y, "rep", over_y)
    near_x, near_y = integrals[:halves], integrals[halves:]
    far_x = lax.ppermute(near_x, "rep", over_x)
    far_y = lax.ppermute(near_y, "rep", over_y)

    def product(parts, cost):
        return pl.pallas_call(
            product_kernel,
            out_shape=(sums, sums),
            in_specs=[in_vmem] * 10,
            out_specs=[in_vmem] * 2,
            scratch_shapes=[VMEM((loops, 4, rows, lanes), bf16)],
            cost_estimate=pl.CostEstimate(flops=cost, bytes_accessed=0, transcendentals=0),
            compiler_params=PARAMS,
        )(*parts, near_x, near_y, far_x, far_y)

    def gathered(mine):
        sibling = lax.ppermute(mine, "loop", over_core)
        three = lax.ppermute(mine, "loop", by_three)
        one = lax.ppermute(jnp.stack([mine, sibling]), "loop", by_core)
        return [mine, sibling, one, lax.ppermute(one, "loop", over_core), three, lax.ppermute(three, "loop", over_core)]

    sent = jnp.concatenate([own[0], lam_x[0][None], lam_y[0][None]], axis=0)
    kept = jnp.concatenate([own[1], lam_x[1][None], lam_y[1][None]], axis=0)
    sent_parts = gathered(sent)
    kept, sent_parts[SENT_FIRST] = lax.optimization_barrier((kept, sent_parts[SENT_FIRST]))
    kept_parts = gathered(kept)
    partial_y, partial_x = product(sent_parts, COST_SENT)
    sum_y = lax.ppermute(partial_y, "rep", over_y)
    sum_x = lax.ppermute(partial_x, "rep", over_x)
    kept_parts, partial_y = lax.optimization_barrier((kept_parts, partial_y))
    own_y, own_x = product(kept_parts, COST_KEPT)
    return pl.pallas_call(
        total_kernel,
        out_shape=jax.ShapeDtypeStruct((irreps, rows, columns), bf16),
        in_specs=[in_vmem] * 4,
        out_specs=in_vmem,
        compiler_params=PARAMS,
    )(own_y, own_x, sum_y, sum_x)


def general(lam, integrals, block_mask):
    live = jnp.repeat(block_mask, lam.shape[2], axis=1) == 1
    kept = jnp.where(live[:, :, None], integrals, jnp.zeros_like(integrals))
    layer_lam = lax.all_gather(lam, "loop", axis=2, tiled=True)
    partial_sum = jnp.einsum("hpk,hka->hpa", layer_lam, kept, preferred_element_type=jnp.float32)
    return lax.psum_scatter(partial_sum, "rep", scatter_dimension=1, tiled=True).astype(jnp.bfloat16)


SENT_FIRST, COST_SENT, COST_KEPT = 4, 0, 0


def solution(mesh):
    return jax.shard_map(
        square if (mesh.shape["rep"], mesh.shape["loop"]) == (4, 2 * CHIPS) else general,
        mesh=mesh,
        in_specs=(P(None, None, ("rep", "loop")), P(None, "rep", "loop"), P(None, "rep")),
        out_specs=P(None, "rep", "loop"),
        check_vma=False,
    )
```

```python
import functools

import jax
import jax.numpy as jnp
from jax import lax
from jax.experimental import pallas as pl
from jax.experimental.pallas import tpu as pltpu
from jax.sharding import PartitionSpec as P

VMEM = pltpu.VMEM
ALONE, BY_CORE = 3, (1, 2)
PARAMS = pltpu.CompilerParams(vmem_limit_bytes=16 << 20)
CHIPS = 4
COST_PACK, COST_JOIN, COST_SENT, COST_KEPT, TIES, CUT_SENT, CUT_KEPT, KTIE, OTIE = 2 * 10**9, 2 * 10**9, 0, 0, 2, 1, 1, 0, 1


def cost(flops):
    return pl.CostEstimate(flops=flops, bytes_accessed=0, transcendentals=0)


def swap(array, pairs, scope):
    with jax.named_scope(scope):
        return lax.ppermute(array, ("loop", "rep"), pairs)


def position():
    rep, spot = lax.axis_index("rep"), lax.axis_index("loop")
    return rep // 2, rep % 2, spot // 2, spot % 2


def pack_kernel(halves, lam_ref, mine_ref, other_ref, to_mine_ref, to_other_ref, turned):
    y, x, _, core = position()
    rows = turned.shape[2]
    for kind in range(2):
        block = jnp.concatenate([lam_ref[kind * halves + h] for h in range(halves)], axis=0)
        flipped = block.T
        for quarter in range(4):
            turned[kind, quarter] = flipped[quarter * rows : (quarter + 1) * rows]
    kept, over_x, over_y, over_both = y * 2 + x, y * 2 + 1 - x, (1 - y) * 2 + x, (1 - y) * 2 + 1 - x
    for kind, own_ref, to_ref in ((core, mine_ref, to_mine_ref), (1 - core, other_ref, to_other_ref)):
        summed, fetched = jnp.where(kind == 0, over_y, over_x), jnp.where(kind == 0, over_x, over_y)
        own_ref[0] = turned[kind, summed]
        own_ref[1] = turned[kind, kept]
        to_ref[0] = turned[kind, over_both]
        to_ref[1] = turned[kind, fetched]


def split_kernel(mask_ref, integrals_ref, _, mine_ref, other_ref):
    irreps, blocks = mask_ref.shape
    halves = irreps // 2
    rows = integrals_ref.shape[1] // blocks
    core = position()[3]
    for kind, out_ref in ((core, mine_ref), (1 - core, other_ref)):
        for h in range(halves):
            for b in range(blocks):
                part = integrals_ref[kind * halves + h, b * rows : (b + 1) * rows]
                live = mask_ref[kind * halves + h, b] == 1
                out_ref[h, b * rows : (b + 1) * rows] = jnp.where(live, part, jnp.zeros_like(part))


def join_kernel(mine_ref, other_ref, far_mine_ref, far_other_ref, sent_ref, kept_ref):
    for which, out_ref in enumerate((sent_ref, kept_ref)):
        for slot, ref in enumerate((mine_ref, other_ref, far_mine_ref, far_other_ref)):
            out_ref[slot] = ref[which]


def product_kernel(
    own_ref, sibling_ref, one_ref, two_ref, alone_ref, alone_sibling_ref,
    near_ref, near_other_ref, far_ref, far_other_ref, out_ref, out_other_ref, pieces,
):
    _, _, z, core = position()

    def place(message, back, from_sibling):
        block = (z ^ back) * 2 + (1 - core if from_sibling else core)
        for layer in range(2):
            for kind in range(2):
                pieces[layer, kind, block] = message[2 * layer + (1 - kind if from_sibling else kind)]

    held = jnp.where(core == 0, BY_CORE[0], BY_CORE[1])
    passed = jnp.where(core == 0, BY_CORE[1], BY_CORE[0])
    place(own_ref[...], 0, False)
    place(sibling_ref[...], 0, True)
    place(alone_ref[...], ALONE, False)
    place(alone_sibling_ref[...], ALONE, True)
    place(one_ref[0], held, False)
    place(one_ref[1], held, True)
    place(two_ref[0], passed, True)
    place(two_ref[1], passed, False)
    halves = near_ref.shape[0]
    depth = pieces.shape[4] // halves
    for kind, (near, far, out) in enumerate(((near_ref, far_ref, out_ref), (near_other_ref, far_other_ref, out_other_ref))):
        parts = [[pieces[layer, kind, s] for s in range(2 * CHIPS)] for layer in range(2)]
        for h in range(halves):
            cut = slice(h * depth, (h + 1) * depth)
            near_lam, far_lam = (jnp.concatenate([p[:, cut] for p in parts[layer]], axis=1) for layer in range(2))
            out[h] = jnp.dot(near_lam, near[h], preferred_element_type=jnp.float32) + jnp.dot(
                far_lam, far[h], preferred_element_type=jnp.float32
            )


def total_kernel(mine_ref, other_ref, sum_mine_ref, sum_other_ref, out_ref):
    halves = mine_ref.shape[0]
    core = position()[3]
    out_ref[pl.ds(core * halves, halves)] = (mine_ref[...] + sum_mine_ref[...]).astype(out_ref.dtype)
    out_ref[pl.ds((1 - core) * halves, halves)] = (other_ref[...] + sum_other_ref[...]).astype(out_ref.dtype)


def square(lam, integrals, block_mask):
    irreps, occ, depth = lam.shape
    halves = irreps // 2
    rows = occ // 4
    columns = integrals.shape[2]
    loops = 2 * CHIPS
    bf16, f32 = jnp.bfloat16, jnp.float32
    lanes = halves * depth
    in_vmem = pl.BlockSpec(memory_space=VMEM)
    quarters = jax.ShapeDtypeStruct((2, rows, lanes), bf16)
    half = jax.ShapeDtypeStruct((halves,) + integrals.shape[1:], bf16)
    sums = jax.ShapeDtypeStruct((halves, rows, columns), f32)

    def pairs(aim):
        places = [(s, r) for s in range(loops) for r in range(4)]
        return [(at, places.index(aim(s, r, s % 2))) for at, (s, r) in enumerate(places)]

    over_core = pairs(lambda s, r, core: (s ^ 1, r))
    fetch = pairs(lambda s, r, core: (s, r ^ (1 + core)))
    reduce = pairs(lambda s, r, core: (s, r ^ (2 - core)))
    by_three = pairs(lambda s, r, core: (s ^ (2 * ALONE), r))
    by_core = pairs(lambda s, r, core: (s ^ (2 * BY_CORE[core]), r))

    mine, other, to_mine, to_other = pl.pallas_call(
        functools.partial(pack_kernel, halves),
        out_shape=[quarters] * 4,
        in_specs=[in_vmem],
        out_specs=[in_vmem] * 4,
        scratch_shapes=[VMEM((2, 4, rows, lanes), bf16)],
        cost_estimate=cost(COST_PACK),
        compiler_params=PARAMS,
    )(lam.transpose(0, 2, 1))
    far_mine = swap(to_mine, fetch, "lam_mine")
    far_other = swap(to_other, reduce, "lam_other")

    near, near_other = pl.pallas_call(
        split_kernel,
        out_shape=[half] * 2,
        in_specs=[pl.BlockSpec(memory_space=pltpu.SMEM), in_vmem, pl.BlockSpec(memory_space=pl.ANY)],
        out_specs=[in_vmem] * 2,
        compiler_params=PARAMS,
    )(block_mask, integrals, to_mine)
    far = swap(near, fetch, "integrals_mine")
    far_other_integrals = swap(near_other, reduce, "integrals_other")

    starts = pl.pallas_call(
        join_kernel,
        out_shape=[jax.ShapeDtypeStruct((4, rows, lanes), bf16)] * 2,
        in_specs=[in_vmem] * 4,
        out_specs=[in_vmem] * 2,
        cost_estimate=cost(COST_JOIN),
        compiler_params=PARAMS,
    )(mine, other, far_mine, far_other)

    def gathered(which, name):
        own = starts[which]
        sibling = swap(own, over_core, name + "_own_over_core")
        return own, sibling, swap(own, by_three, name + "_by_three")

    def with_core(parts, name):
        own, sibling, three = parts
        return [own, sibling, swap(jnp.stack([own, sibling]), by_core, name + "_by_core"), three]

    def exchanged(parts, name):
        own, sibling, one, three = parts
        three_sibling = swap(three, over_core, name + "_three_over_core")
        if name == "sent":
            one, three_sibling = lax.optimization_barrier((one, three_sibling))
        cut = CUT_SENT if name == "sent" else CUT_KEPT
        two = jnp.concatenate([swap(part, over_core, name + "_one_over_core") for part in jnp.split(one, cut, axis=1)], axis=1)
        return [own, sibling, one, two, three, three_sibling]

    def product(parts, flops):
        return pl.pallas_call(
            product_kernel,
            out_shape=[sums] * 2,
            in_specs=[in_vmem] * 10,
            out_specs=[in_vmem] * 2,
            scratch_shapes=[VMEM((2, 2, loops, rows, lanes), bf16)],
            cost_estimate=cost(flops),
            compiler_params=PARAMS,
        )(*parts, near, near_other, far, far_other_integrals)

    sent_parts = gathered(0, "sent")
    kept_own, kept_sibling, kept_three = gathered(1, "kept")
    sent_parts = with_core(sent_parts, "sent")
    if OTIE == 1:
        sent_parts[3], kept_sibling = lax.optimization_barrier((sent_parts[3], kept_sibling))
    if KTIE == 1:
        sent_parts[2], kept_three = lax.optimization_barrier((sent_parts[2], kept_three))
    kept_parts = with_core((kept_own, kept_sibling, kept_three), "kept")
    if TIES == 1:
        sent_parts[2], far, far_other_integrals = lax.optimization_barrier((sent_parts[2], far, far_other_integrals))
    if TIES == 2:
        sent_parts[3], far, far_other_integrals = lax.optimization_barrier((sent_parts[3], far, far_other_integrals))
    sent, sent_other = product(exchanged(sent_parts, "sent"), COST_SENT)
    sum_mine = swap(sent, reduce, "sums_mine")
    sum_other = swap(sent_other, fetch, "sums_other")
    kept_parts, sent = lax.optimization_barrier((kept_parts, sent))
    kept, kept_other = product(exchanged(kept_parts, "kept"), COST_KEPT)
    return pl.pallas_call(
        total_kernel,
        out_shape=jax.ShapeDtypeStruct((irreps, rows, columns), bf16),
        in_specs=[in_vmem] * 4,
        out_specs=in_vmem,
        compiler_params=PARAMS,
    )(kept, kept_other, sum_mine, sum_other)


def general(lam, integrals, block_mask):
    live = jnp.repeat(block_mask, lam.shape[2], axis=1) == 1
    kept = jnp.where(live[:, :, None], integrals, jnp.zeros_like(integrals))
    layer_lam = lax.all_gather(lam, "loop", axis=2, tiled=True)
    partial_sum = jnp.einsum("hpk,hka->hpa", layer_lam, kept, preferred_element_type=jnp.float32)
    return lax.psum_scatter(partial_sum, "rep", scatter_dimension=1, tiled=True).astype(jnp.bfloat16)


def solution(mesh):
    return jax.shard_map(
        square if (mesh.shape["rep"], mesh.shape["loop"]) == (4, 2 * CHIPS) else general,
        mesh=mesh,
        in_specs=(P(None, None, ("rep", "loop")), P(None, "rep", "loop"), P(None, "rep")),
        out_specs=P(None, "rep", "loop"),
        check_vma=False,
    )
```

```python
import functools

import jax
import jax.numpy as jnp
from jax import lax
from jax.experimental import pallas as pl
from jax.experimental.pallas import tpu as pltpu
from jax.sharding import PartitionSpec as P

VMEM = pltpu.VMEM
SENT, KEPT = (3, 1, 2), (3, 1, 2)
PARAMS = pltpu.CompilerParams(vmem_limit_bytes=16 << 20)
CHIPS = 4
COST_PACK, COST_JOIN, COST_FAR = 2 * 10**9, 4 * 10**9, 4 * 10**9
COST_SENT, COST_OTHER, COST_KEPT, COST_SUM, HOLD, APART = 0, 0, 0, 2 * 10**9, 0, 1


def cost(flops):
    return pl.CostEstimate(flops=flops, bytes_accessed=0, transcendentals=0)


def swap(array, pairs, scope):
    with jax.named_scope(scope):
        return lax.ppermute(array, ("loop", "rep"), pairs)


def mark(flops, *arrays):
    return pl.pallas_call(
        lambda *refs: None,
        out_shape=[jax.ShapeDtypeStruct(array.shape, array.dtype) for array in arrays],
        in_specs=[pl.BlockSpec(memory_space=VMEM)] * len(arrays),
        out_specs=[pl.BlockSpec(memory_space=VMEM)] * len(arrays),
        input_output_aliases={i: i for i in range(len(arrays))},
        cost_estimate=cost(flops),
        compiler_params=PARAMS,
    )(*arrays)


def position():
    rep, spot = lax.axis_index("rep"), lax.axis_index("loop")
    return rep // 2, rep % 2, spot // 2, spot % 2


def pack_kernel(halves, lam_ref, mine_ref, other_ref, to_mine_ref, to_other_ref, turned):
    y, x, _, core = position()
    rows = turned.shape[2]
    for kind in range(2):
        block = jnp.concatenate([lam_ref[kind * halves + h] for h in range(halves)], axis=0)
        flipped = block.T
        for quarter in range(4):
            turned[kind, quarter] = flipped[quarter * rows : (quarter + 1) * rows]
    kept, over_x, over_y, over_both = y * 2 + x, y * 2 + 1 - x, (1 - y) * 2 + x, (1 - y) * 2 + 1 - x
    for kind, own_ref, to_ref in ((core, mine_ref, to_mine_ref), (1 - core, other_ref, to_other_ref)):
        summed, fetched = jnp.where(kind == 0, over_y, over_x), jnp.where(kind == 0, over_x, over_y)
        own_ref[0] = turned[kind, summed]
        own_ref[1] = turned[kind, kept]
        to_ref[0] = turned[kind, over_both]
        to_ref[1] = turned[kind, fetched]


def split_kernel(mask_ref, integrals_ref, _, mine_ref, other_ref):
    irreps, blocks = mask_ref.shape
    halves = irreps // 2
    _, depth, columns = integrals_ref.shape
    core = position()[3]
    for kind, out_ref in ((core, mine_ref), (1 - core, other_ref)):
        live = mask_ref[pl.ds(kind * halves, halves)].astype(jnp.float32)
        for h in range(halves):
            for b in range(blocks):
                rows = slice(b * depth // blocks, (b + 1) * depth // blocks)
                factor = jnp.broadcast_to(live[h : h + 1, b : b + 1], (depth // blocks, columns)).astype(jnp.bfloat16)
                out_ref[h, rows] = integrals_ref[kind * halves + h, rows] * factor


def join_kernel(mine_ref, other_ref, far_mine_ref, far_other_ref, sent_ref, kept_ref):
    for which, out_ref in enumerate((sent_ref, kept_ref)):
        for slot, ref in enumerate((mine_ref, other_ref, far_mine_ref, far_other_ref)):
            out_ref[slot] = ref[which]


def product_kernel(kinds, hops, *refs):
    own_ref, sibling_ref, one_ref, two_ref, alone_ref, alone_sibling_ref = refs[:6]
    integrals_refs, out_refs, pieces = refs[6 : 6 + 2 * len(kinds)], refs[6 + 2 * len(kinds) : -1], refs[-1]
    _, _, z, core = position()

    def place(message, back, from_sibling):
        block = (z ^ back) * 2 + (1 - core if from_sibling else core)
        for layer in range(2):
            for slot, kind in enumerate(kinds):
                pieces[layer, slot, block] = message[2 * layer + (1 - kind if from_sibling else kind)]

    held = jnp.where(core == 0, hops[1], hops[2])
    passed = jnp.where(core == 0, hops[2], hops[1])
    place(own_ref, 0, False)
    place(sibling_ref, 0, True)
    place(alone_ref, hops[0], False)
    place(alone_sibling_ref, hops[0], True)
    place(one_ref.at[0], held, False)
    place(one_ref.at[1], held, True)
    place(two_ref.at[0], passed, True)
    place(two_ref.at[1], passed, False)
    for slot, out in enumerate(out_refs):
        near, far = integrals_refs[2 * slot : 2 * slot + 2]
        halves = near.shape[0]
        depth = pieces.shape[4] // halves
        parts = [[pieces[layer, slot, s] for s in range(2 * CHIPS)] for layer in range(2)]
        for h in range(halves):
            cut = slice(h * depth, (h + 1) * depth)
            near_lam, far_lam = (jnp.concatenate([p[:, cut] for p in parts[layer]], axis=1) for layer in range(2))
            out[h] = jnp.dot(near_lam, near[h], preferred_element_type=jnp.float32) + jnp.dot(
                far_lam, far[h], preferred_element_type=jnp.float32
            )


def total_kernel(kept_ref, kept_other_ref, arrived_ref, arrived_other_ref, out_ref, rounded, done):
    core = position()[3]
    halves = kept_ref.shape[0]
    copies = []
    for kind, kept, arrived in ((0, kept_ref, arrived_ref), (1, kept_other_ref, arrived_other_ref)):
        at = (1 - core if kind else core) * halves
        for h in range(halves):
            step = kind * halves + h
            rounded[step] = (kept[h] + arrived[h]).astype(rounded.dtype)
            copies.append(pltpu.make_async_copy(rounded.at[step], out_ref.at[at + h], done.at[step]))
            copies[-1].start()
    for copy in copies:
        copy.wait()


def square(lam, integrals, block_mask):
    irreps, occ, depth = lam.shape
    halves = irreps // 2
    rows = occ // 4
    columns = integrals.shape[2]
    loops = 2 * CHIPS
    bf16, f32 = jnp.bfloat16, jnp.float32
    lanes = halves * depth
    in_vmem = pl.BlockSpec(memory_space=VMEM)
    quarters = jax.ShapeDtypeStruct((2, rows, lanes), bf16)
    half = jax.ShapeDtypeStruct((halves,) + integrals.shape[1:], bf16)
    sums = jax.ShapeDtypeStruct((halves, rows, columns), f32)

    def pairs(aim):
        places = [(s, r) for s in range(loops) for r in range(4)]
        return [(at, places.index(aim(s, r, s % 2))) for at, (s, r) in enumerate(places)]

    over_core = pairs(lambda s, r, core: (s ^ 1, r))
    fetch = pairs(lambda s, r, core: (s, r ^ (1 + core)))
    reduce = pairs(lambda s, r, core: (s, r ^ (2 - core)))
    alone = lambda hops: pairs(lambda s, r, core: (s ^ (2 * hops[0]), r))
    by_core = lambda hops: pairs(lambda s, r, core: (s ^ (2 * hops[1 + core]), r))

    mine, other, to_mine, to_other = pl.pallas_call(
        functools.partial(pack_kernel, halves),
        out_shape=[quarters] * 4,
        in_specs=[in_vmem],
        out_specs=[in_vmem] * 4,
        scratch_shapes=[VMEM((2, 4, rows, lanes), bf16)],
        cost_estimate=cost(COST_PACK),
        compiler_params=PARAMS,
    )(lam.transpose(0, 2, 1))
    far_mine = swap(to_mine, fetch, "lam_mine")
    far_other = swap(to_other, reduce, "lam_other")

    near, near_other = pl.pallas_call(
        split_kernel,
        out_shape=[half] * 2,
        in_specs=[in_vmem, in_vmem, pl.BlockSpec(memory_space=pl.ANY)],
        out_specs=[in_vmem] * 2,
        compiler_params=PARAMS,
    )(block_mask, integrals, to_mine)
    far = swap(near, fetch, "integrals_mine")
    far_other_integrals = swap(near_other, reduce, "integrals_other")

    starts = pl.pallas_call(
        join_kernel,
        out_shape=[jax.ShapeDtypeStruct((4, rows, lanes), bf16)] * 2,
        in_specs=[in_vmem] * 4,
        out_specs=[in_vmem] * 2,
        cost_estimate=cost(COST_JOIN),
        compiler_params=PARAMS,
    )(mine, other, far_mine, far_other)

    def gathered(which, hops, name):
        own = starts[which]
        sibling = swap(own, over_core, name + "_own_over_core")
        return own, sibling, swap(own, alone(hops), name + "_by_three")

    def with_core(parts, hops, name):
        own, sibling, three = parts
        return [own, sibling, swap(jnp.stack([own, sibling]), by_core(hops), name + "_by_core"), three]

    def exchanged(parts, name):
        own, sibling, one, three = parts
        three_sibling = swap(three, over_core, name + "_three_over_core")
        if name == "sent":
            one, three_sibling = lax.optimization_barrier((one, three_sibling))
        return [own, sibling, one, swap(one, over_core, name + "_one_over_core"), three, three_sibling]

    def product(parts, kinds, hops, flops):
        given = [(near, far), (near_other, far_other_integrals)]
        return pl.pallas_call(
            functools.partial(product_kernel, kinds, hops),
            out_shape=[sums] * len(kinds),
            in_specs=[in_vmem] * (6 + 2 * len(kinds)),
            out_specs=[in_vmem] * len(kinds),
            scratch_shapes=[VMEM((2, len(kinds), loops, rows, lanes), bf16)],
            cost_estimate=cost(flops),
            compiler_params=PARAMS,
        )(*parts, *(array for kind in kinds for array in given[kind]))

    sent_parts = with_core(gathered(0, SENT, "sent"), SENT, "sent")
    kept_own = starts[1]
    kept_sibling = swap(kept_own, over_core, "kept_own_over_core")
    sent_parts[3], kept_sibling = lax.optimization_barrier((sent_parts[3], kept_sibling))
    alone_own = kept_own
    if HOLD == 1:
        sent_parts[2], alone_own = lax.optimization_barrier((sent_parts[2], alone_own))
    if HOLD == 2:
        sent_parts[2], kept_sibling = lax.optimization_barrier((sent_parts[2], kept_sibling))
    far, far_other_integrals = mark(COST_FAR, far, far_other_integrals)
    if HOLD == 3:
        far, alone_own = lax.optimization_barrier((far, alone_own))
    kept_alone = swap(alone_own, alone(KEPT), "kept_by_three")
    kept_parts = with_core((kept_own, kept_sibling, kept_alone), KEPT, "kept")
    sent_parts = exchanged(sent_parts, "sent")
    if APART:
        (sent,) = product(sent_parts, (0,), SENT, COST_SENT)
        (sent_other,) = product(sent_parts, (1,), SENT, COST_OTHER)
    else:
        sent, sent_other = product(sent_parts, (0, 1), SENT, COST_SENT)
    sum_mine = swap(sent, reduce, "sums_mine")
    sum_other = swap(sent_other, fetch, "sums_other")
    if COST_SUM:
        (sum_mine,) = mark(COST_SUM, sum_mine)
    kept_parts, sent = lax.optimization_barrier((kept_parts, sent))
    kept, kept_other = product(exchanged(kept_parts, "kept"), (0, 1), KEPT, COST_KEPT)
    return pl.pallas_call(
        total_kernel,
        out_shape=jax.ShapeDtypeStruct((irreps, rows, columns), bf16),
        in_specs=[in_vmem] * 4,
        out_specs=pl.BlockSpec(memory_space=pl.ANY),
        scratch_shapes=[VMEM((irreps, rows, columns), bf16), pltpu.SemaphoreType.DMA((irreps,))],
        compiler_params=PARAMS,
    )(kept, kept_other, sum_mine, sum_other)


def general(lam, integrals, block_mask):
    live = jnp.repeat(block_mask, lam.shape[2], axis=1) == 1
    kept = jnp.where(live[:, :, None], integrals, jnp.zeros_like(integrals))
    layer_lam = lax.all_gather(lam, "loop", axis=2, tiled=True)
    partial_sum = jnp.einsum("hpk,hka->hpa", layer_lam, kept, preferred_element_type=jnp.float32)
    return lax.psum_scatter(partial_sum, "rep", scatter_dimension=1, tiled=True).astype(jnp.bfloat16)


def solution(mesh):
    return jax.shard_map(
        square if (mesh.shape["rep"], mesh.shape["loop"]) == (4, 2 * CHIPS) else general,
        mesh=mesh,
        in_specs=(P(None, None, ("rep", "loop")), P(None, "rep", "loop"), P(None, "rep")),
        out_specs=P(None, "rep", "loop"),
        check_vma=False,
    )
```

```python
import functools

import jax
import jax.numpy as jnp
from jax import lax
from jax.experimental import pallas as pl
from jax.experimental.pallas import tpu as pltpu
from jax.sharding import PartitionSpec as P

VMEM = pltpu.VMEM
SENT, KEPT = (3, 1, 2), (1, 3, 2)
PARAMS = pltpu.CompilerParams(vmem_limit_bytes=16 << 20)
CHIPS = 4
COST_PACK, COST_JOIN, COST_FAR, COST_FAR_OTHER = 2 * 10**9, 4 * 10**9, 4 * 10**9, 2 * 10**9
COST_SENT, COST_OTHER, COST_KEPT, COST_SUM, TIE_NEAR = 0, 0, 0, 0, 1


def cost(flops):
    return pl.CostEstimate(flops=flops, bytes_accessed=0, transcendentals=0)


def swap(array, pairs, scope):
    with jax.named_scope(scope):
        return lax.ppermute(array, ("loop", "rep"), pairs)


def mark(flops, *arrays):
    return pl.pallas_call(
        lambda *refs: None,
        out_shape=[jax.ShapeDtypeStruct(array.shape, array.dtype) for array in arrays],
        in_specs=[pl.BlockSpec(memory_space=VMEM)] * len(arrays),
        out_specs=[pl.BlockSpec(memory_space=VMEM)] * len(arrays),
        input_output_aliases={i: i for i in range(len(arrays))},
        cost_estimate=cost(flops),
        compiler_params=PARAMS,
    )(*arrays)


def position():
    rep, spot = lax.axis_index("rep"), lax.axis_index("loop")
    return rep // 2, rep % 2, spot // 2, spot % 2


def pack_kernel(halves, lam_ref, sent_ref, kept_ref, to_mine_ref, to_other_ref, turned):
    y, x, _, core = position()
    rows = turned.shape[2]
    for kind in range(2):
        block = jnp.concatenate([lam_ref[kind * halves + h] for h in range(halves)], axis=0)
        flipped = block.T
        for quarter in range(4):
            turned[kind, quarter] = flipped[quarter * rows : (quarter + 1) * rows]
    kept, over_x, over_y, over_both = y * 2 + x, y * 2 + 1 - x, (1 - y) * 2 + x, (1 - y) * 2 + 1 - x
    for slot, (kind, to_ref) in enumerate(((core, to_mine_ref), (1 - core, to_other_ref))):
        summed, fetched = jnp.where(kind == 0, over_y, over_x), jnp.where(kind == 0, over_x, over_y)
        sent_ref[slot] = turned[kind, summed]
        kept_ref[slot] = turned[kind, kept]
        to_ref[0] = turned[kind, over_both]
        to_ref[1] = turned[kind, fetched]


def split_kernel(mask_ref, integrals_ref, _, mine_ref, other_ref):
    irreps, blocks = mask_ref.shape
    halves = irreps // 2
    _, depth, columns = integrals_ref.shape
    core = position()[3]
    for kind, out_ref in ((core, mine_ref), (1 - core, other_ref)):
        live = mask_ref[pl.ds(kind * halves, halves)].astype(jnp.float32)
        for h in range(halves):
            for b in range(blocks):
                rows = slice(b * depth // blocks, (b + 1) * depth // blocks)
                factor = jnp.broadcast_to(live[h : h + 1, b : b + 1], (depth // blocks, columns)).astype(jnp.bfloat16)
                out_ref[h, rows] = integrals_ref[kind * halves + h, rows] * factor


def join_kernel(sent_own_ref, kept_own_ref, far_mine_ref, far_other_ref, sent_ref, sent_far_ref, kept_ref):
    for which, (own_ref, out_ref) in enumerate(((sent_own_ref, sent_ref), (kept_own_ref, kept_ref))):
        for slot, ref in enumerate((far_mine_ref, far_other_ref)):
            out_ref[slot] = own_ref[slot]
            out_ref[2 + slot] = ref[which]
    sent_far_ref[0] = far_mine_ref[0]
    sent_far_ref[1] = far_other_ref[0]


def product_kernel(kinds, hops, held, names, *refs):
    count = len(names)
    messages, integrals_refs, rest = dict(zip(names, refs)), refs[count : count + 2 * len(kinds)], refs[count + 2 * len(kinds) :]
    before, out_refs = (rest[: len(kinds)], rest[len(kinds) :]) if held else (None, rest)
    _, _, z, core = position()
    by_core = jnp.where(core == 0, hops[1], hops[2])
    passed = jnp.where(core == 0, hops[2], hops[1])
    parts = []
    for name, ref in messages.items():
        layers = (0,) if "near" in name else (1,) if "far" in name else (0, 1)
        if "one" in name.split("_"):
            parts += [(ref.at[0], by_core, False, layers), (ref.at[1], by_core, True, layers)]
        elif "two" in name:
            parts += [(ref.at[0], passed, True, layers), (ref.at[1], passed, False, layers)]
        else:
            parts.append((ref, hops[0] if "alone" in name else 0, "sibling" in name, layers))
    for slot, kind in enumerate(kinds):
        integrals = integrals_refs[2 * slot : 2 * slot + 2]
        halves = integrals[0].shape[0]
        depth = messages[names[0]].shape[-1] // halves
        for h in range(halves):
            lam, kept = [], []
            for layer in range(2):
                for ref, hop, from_sibling, layers in parts:
                    if layer in layers:
                        block = (z ^ hop) * 2 + (1 - core if from_sibling else core)
                        unit = 2 * layers.index(layer) + (1 - kind if from_sibling else kind)
                        lam.append(ref[unit][:, h * depth : (h + 1) * depth])
                        kept.append(integrals[layer][h, pl.ds(pl.multiple_of(block * depth, depth), depth)])
            value = jnp.dot(
                jnp.concatenate(lam, axis=1), jnp.concatenate(kept, axis=0), preferred_element_type=jnp.float32
            )
            out_refs[slot][h] = before[slot][h] + value if held else value


def total_kernel(kept_ref, kept_other_ref, arrived_ref, arrived_other_ref, out_ref, rounded, done):
    core = position()[3]
    halves = kept_ref.shape[0]
    copies = []
    for kind, kept, arrived in ((0, kept_ref, arrived_ref), (1, kept_other_ref, arrived_other_ref)):
        at = (1 - core if kind else core) * halves
        for h in range(halves):
            step = kind * halves + h
            rounded[step] = (kept[h] + arrived[h]).astype(rounded.dtype)
            copies.append(pltpu.make_async_copy(rounded.at[step], out_ref.at[at + h], done.at[step]))
            copies[-1].start()
    for copy in copies:
        copy.wait()


def square(lam, integrals, block_mask):
    irreps, occ, depth = lam.shape
    halves = irreps // 2
    rows = occ // 4
    columns = integrals.shape[2]
    loops = 2 * CHIPS
    bf16, f32 = jnp.bfloat16, jnp.float32
    lanes = halves * depth
    in_vmem = pl.BlockSpec(memory_space=VMEM)
    quarters = jax.ShapeDtypeStruct((2, rows, lanes), bf16)
    half = jax.ShapeDtypeStruct((halves,) + integrals.shape[1:], bf16)
    sums = jax.ShapeDtypeStruct((halves, rows, columns), f32)

    def pairs(aim):
        places = [(s, r) for s in range(loops) for r in range(4)]
        return [(at, places.index(aim(s, r, s % 2))) for at, (s, r) in enumerate(places)]

    over_core = pairs(lambda s, r, core: (s ^ 1, r))
    fetch = pairs(lambda s, r, core: (s, r ^ (1 + core)))
    reduce = pairs(lambda s, r, core: (s, r ^ (2 - core)))
    alone = lambda hops: pairs(lambda s, r, core: (s ^ (2 * hops[0]), r))
    by_core = lambda hops: pairs(lambda s, r, core: (s ^ (2 * hops[1 + core]), r))

    sent_own, kept_own, to_mine, to_other = pl.pallas_call(
        functools.partial(pack_kernel, halves),
        out_shape=[quarters] * 4,
        in_specs=[in_vmem],
        out_specs=[in_vmem] * 4,
        scratch_shapes=[VMEM((2, 4, rows, lanes), bf16)],
        cost_estimate=cost(COST_PACK),
        compiler_params=PARAMS,
    )(lam.transpose(0, 2, 1))
    far_mine = swap(to_mine, fetch, "lam_mine")
    far_other = swap(to_other, reduce, "lam_other")

    near_sibling = swap(sent_own, over_core, "sent_near_over_core")
    one_near = swap(jnp.stack([sent_own, near_sibling]), by_core(SENT), "sent_near_by_core")

    near, near_other = pl.pallas_call(
        split_kernel,
        out_shape=[half] * 2,
        in_specs=[in_vmem, in_vmem, pl.BlockSpec(memory_space=pl.ANY)],
        out_specs=[in_vmem] * 2,
        compiler_params=PARAMS,
    )(block_mask, integrals, to_mine)
    far = swap(near, fetch, "integrals_mine")
    if TIE_NEAR == 1:
        near_other, one_near = lax.optimization_barrier((near_other, one_near))
    far_other_integrals = swap(near_other, reduce, "integrals_other")

    message = jax.ShapeDtypeStruct((4, rows, lanes), bf16)
    sent, sent_far, kept = pl.pallas_call(
        join_kernel,
        out_shape=[message, quarters, message],
        in_specs=[in_vmem] * 4,
        out_specs=[in_vmem] * 3,
        cost_estimate=cost(COST_JOIN),
        compiler_params=PARAMS,
    )(sent_own, kept_own, far_mine, far_other)

    def over_cores(array, scope):
        return swap(array, over_core, scope + "_over_core")

    def for_chip(own, sibling, hops, scope):
        return swap(jnp.stack([own, sibling]), by_core(hops), scope + "_by_core")

    def product(parts, kinds, hops, flops, before=()):
        given = [(near, far), (near_other, far_other_integrals)]
        return pl.pallas_call(
            functools.partial(product_kernel, kinds, hops, bool(before), tuple(parts)),
            out_shape=[sums] * len(kinds),
            in_specs=[in_vmem] * (len(parts) + 2 * len(kinds) + len(before)),
            out_specs=[in_vmem] * len(kinds),
            cost_estimate=cost(flops),
            compiler_params=PARAMS,
        )(*parts.values(), *(array for kind in kinds for array in given[kind]), *before)

    parts = dict(own=sent, sibling_near=near_sibling)
    parts["sibling_far"] = over_cores(sent_far, "sent_far")
    parts["alone"] = swap(sent, alone(SENT), "sent_alone")
    parts["one_far"] = for_chip(sent_far, parts["sibling_far"], SENT, "sent_far")
    kept_sibling = over_cores(kept, "kept")
    parts["alone"], kept_sibling = lax.optimization_barrier((parts["alone"], kept_sibling))
    kept_parts = dict(own=kept, sibling=kept_sibling)
    kept_parts["one"] = for_chip(kept, kept_sibling, KEPT, "kept")
    if COST_FAR:
        (far,) = mark(COST_FAR, far)
    if COST_FAR_OTHER:
        (far_other_integrals,) = mark(COST_FAR_OTHER, far_other_integrals)
    parts["alone_sibling"] = over_cores(parts["alone"], "sent_alone")
    parts["one_far"], parts["alone_sibling"] = lax.optimization_barrier((parts["one_far"], parts["alone_sibling"]))
    parts["one_near"], parts["two_near"] = one_near, over_cores(one_near, "sent_near_one")
    last = dict(two_far=over_cores(parts["one_far"], "sent_far_one"))
    sent_parts = parts
    (sent,) = product(last, (0,), SENT, COST_SENT, product(sent_parts, (0,), SENT, COST_SENT))
    (first_other,) = product(sent_parts, (1,), SENT, COST_OTHER)
    kept, first_other = lax.optimization_barrier((kept, first_other))
    kept_parts["alone"] = swap(kept, alone(KEPT), "kept_alone")
    (sent_other,) = product(last, (1,), SENT, COST_OTHER, (first_other,))
    sum_mine = swap(sent, reduce, "sums_mine")
    sum_other = swap(sent_other, fetch, "sums_other")
    if COST_SUM:
        (sum_mine,) = mark(COST_SUM, sum_mine)
    kept_parts, sent = lax.optimization_barrier((kept_parts, sent))
    kept_parts["two"] = over_cores(kept_parts["one"], "kept_one")
    kept_parts["alone_sibling"] = over_cores(kept_parts["alone"], "kept_alone")
    last = {name: kept_parts.pop(name) for name in ("alone", "alone_sibling")}
    kept, kept_other = product(last, (0, 1), KEPT, COST_KEPT, product(kept_parts, (0, 1), KEPT, COST_KEPT))
    return pl.pallas_call(
        total_kernel,
        out_shape=jax.ShapeDtypeStruct((irreps, rows, columns), bf16),
        in_specs=[in_vmem] * 4,
        out_specs=pl.BlockSpec(memory_space=pl.ANY),
        scratch_shapes=[VMEM((irreps, rows, columns), bf16), pltpu.SemaphoreType.DMA((irreps,))],
        compiler_params=PARAMS,
    )(kept, kept_other, sum_mine, sum_other)


def general(lam, integrals, block_mask):
    live = jnp.repeat(block_mask, lam.shape[2], axis=1) == 1
    kept = jnp.where(live[:, :, None], integrals, jnp.zeros_like(integrals))
    layer_lam = lax.all_gather(lam, "loop", axis=2, tiled=True)
    partial_sum = jnp.einsum("hpk,hka->hpa", layer_lam, kept, preferred_element_type=jnp.float32)
    return lax.psum_scatter(partial_sum, "rep", scatter_dimension=1, tiled=True).astype(jnp.bfloat16)


def solution(mesh):
    return jax.shard_map(
        square if (mesh.shape["rep"], mesh.shape["loop"]) == (4, 2 * CHIPS) else general,
        mesh=mesh,
        in_specs=(P(None, None, ("rep", "loop")), P(None, "rep", "loop"), P(None, "rep")),
        out_specs=P(None, "rep", "loop"),
        check_vma=False,
    )
```

```python
import functools

import jax
import jax.numpy as jnp
from jax import lax
from jax.experimental import pallas as pl
from jax.experimental.pallas import tpu as pltpu
from jax.sharding import PartitionSpec as P

VMEM = pltpu.VMEM
SENT, KEPT = (3, 1, 2), (1, 3, 2)
PARAMS = pltpu.CompilerParams(vmem_limit_bytes=16 << 20)
CHIPS = 4
COST_PACK, COST_JOIN, COST_FAR, COST_FAR_OTHER = 2 * 10**9, 4 * 10**9, 4 * 10**9, 2 * 10**9


def cost(flops):
    return pl.CostEstimate(flops=flops, bytes_accessed=0, transcendentals=0)


def swap(array, pairs, scope):
    with jax.named_scope(scope):
        return lax.ppermute(array, ("loop", "rep"), pairs)


def mark(flops, array):
    return pl.pallas_call(
        lambda *refs: None,
        out_shape=jax.ShapeDtypeStruct(array.shape, array.dtype),
        in_specs=[pl.BlockSpec(memory_space=VMEM)],
        out_specs=pl.BlockSpec(memory_space=VMEM),
        input_output_aliases={0: 0},
        cost_estimate=cost(flops),
        compiler_params=PARAMS,
    )(array)


def position():
    rep, spot = lax.axis_index("rep"), lax.axis_index("loop")
    return rep // 2, rep % 2, spot // 2, spot % 2


def pack_kernel(halves, lam_ref, sent_ref, kept_ref, to_mine_ref, to_other_ref, turned):
    y, x, _, core = position()
    rows = turned.shape[2]
    for kind in range(2):
        block = jnp.concatenate([lam_ref[kind * halves + h] for h in range(halves)], axis=0)
        flipped = block.T
        for quarter in range(4):
            turned[kind, quarter] = flipped[quarter * rows : (quarter + 1) * rows]
    kept, over_x, over_y, over_both = y * 2 + x, y * 2 + 1 - x, (1 - y) * 2 + x, (1 - y) * 2 + 1 - x
    for slot, (kind, to_ref) in enumerate(((core, to_mine_ref), (1 - core, to_other_ref))):
        summed, fetched = jnp.where(kind == 0, over_y, over_x), jnp.where(kind == 0, over_x, over_y)
        sent_ref[slot] = turned[kind, summed]
        kept_ref[slot] = turned[kind, kept]
        to_ref[0] = turned[kind, over_both]
        to_ref[1] = turned[kind, fetched]


def split_kernel(mask_ref, integrals_ref, _, mine_ref, other_ref):
    irreps, blocks = mask_ref.shape
    halves = irreps // 2
    _, depth, columns = integrals_ref.shape
    core = position()[3]
    for kind, out_ref in ((core, mine_ref), (1 - core, other_ref)):
        live = mask_ref[pl.ds(kind * halves, halves)].astype(jnp.float32)
        for h in range(halves):
            for b in range(blocks):
                rows = slice(b * depth // blocks, (b + 1) * depth // blocks)
                factor = jnp.broadcast_to(live[h : h + 1, b : b + 1], (depth // blocks, columns)).astype(jnp.bfloat16)
                out_ref[h, rows] = integrals_ref[kind * halves + h, rows] * factor


def join_kernel(sent_own_ref, kept_own_ref, far_mine_ref, far_other_ref, sent_ref, sent_far_ref, kept_ref):
    for which, (own_ref, out_ref) in enumerate(((sent_own_ref, sent_ref), (kept_own_ref, kept_ref))):
        for slot, ref in enumerate((far_mine_ref, far_other_ref)):
            out_ref[slot] = own_ref[slot]
            out_ref[2 + slot] = ref[which]
    sent_far_ref[0] = far_mine_ref[0]
    sent_far_ref[1] = far_other_ref[0]


def product_kernel(kinds, hops, held, names, *refs):
    count = len(names)
    messages, integrals_refs, rest = dict(zip(names, refs)), refs[count : count + 2 * len(kinds)], refs[count + 2 * len(kinds) :]
    before, out_refs = (rest[: len(kinds)], rest[len(kinds) :]) if held else (None, rest)
    _, _, z, core = position()
    by_core = jnp.where(core == 0, hops[1], hops[2])
    passed = jnp.where(core == 0, hops[2], hops[1])
    parts = []
    for name, ref in messages.items():
        layers = (0,) if "near" in name else (1,) if "far" in name else (0, 1)
        if "one" in name.split("_"):
            parts += [(ref.at[0], by_core, False, layers), (ref.at[1], by_core, True, layers)]
        elif "two" in name:
            parts += [(ref.at[0], passed, True, layers), (ref.at[1], passed, False, layers)]
        else:
            parts.append((ref, hops[0] if "alone" in name else 0, "sibling" in name, layers))
    for slot, kind in enumerate(kinds):
        integrals = integrals_refs[2 * slot : 2 * slot + 2]
        halves = integrals[0].shape[0]
        depth = messages[names[0]].shape[-1] // halves
        for h in range(halves):
            lam, kept = [], []
            for layer in range(2):
                for ref, hop, from_sibling, layers in parts:
                    if layer in layers:
                        block = (z ^ hop) * 2 + (1 - core if from_sibling else core)
                        unit = 2 * layers.index(layer) + (1 - kind if from_sibling else kind)
                        lam.append(ref[unit][:, h * depth : (h + 1) * depth])
                        kept.append(integrals[layer][h, pl.ds(pl.multiple_of(block * depth, depth), depth)])
            value = jnp.dot(
                jnp.concatenate(lam, axis=1), jnp.concatenate(kept, axis=0), preferred_element_type=jnp.float32
            )
            out_refs[slot][h] = before[slot][h] + value if held else value


def total_kernel(kept_ref, kept_other_ref, arrived_ref, arrived_other_ref, out_ref, rounded, done):
    core = position()[3]
    halves = kept_ref.shape[0]
    copies = []
    for kind, kept, arrived in ((0, kept_ref, arrived_ref), (1, kept_other_ref, arrived_other_ref)):
        at = (1 - core if kind else core) * halves
        for h in range(halves):
            step = kind * halves + h
            rounded[step] = (kept[h] + arrived[h]).astype(rounded.dtype)
            copies.append(pltpu.make_async_copy(rounded.at[step], out_ref.at[at + h], done.at[step]))
            copies[-1].start()
    for copy in copies:
        copy.wait()


def square(lam, integrals, block_mask):
    irreps, occ, depth = lam.shape
    halves = irreps // 2
    rows = occ // 4
    columns = integrals.shape[2]
    loops = 2 * CHIPS
    bf16, f32 = jnp.bfloat16, jnp.float32
    lanes = halves * depth
    in_vmem = pl.BlockSpec(memory_space=VMEM)
    quarters = jax.ShapeDtypeStruct((2, rows, lanes), bf16)
    half = jax.ShapeDtypeStruct((halves,) + integrals.shape[1:], bf16)
    sums = jax.ShapeDtypeStruct((halves, rows, columns), f32)

    def pairs(aim):
        places = [(s, r) for s in range(loops) for r in range(4)]
        return [(at, places.index(aim(s, r, s % 2))) for at, (s, r) in enumerate(places)]

    over_core = pairs(lambda s, r, core: (s ^ 1, r))
    fetch = pairs(lambda s, r, core: (s, r ^ (1 + core)))
    reduce = pairs(lambda s, r, core: (s, r ^ (2 - core)))
    alone = lambda hops: pairs(lambda s, r, core: (s ^ (2 * hops[0]), r))
    by_core = lambda hops: pairs(lambda s, r, core: (s ^ (2 * hops[1 + core]), r))

    sent_own, kept_own, to_mine, to_other = pl.pallas_call(
        functools.partial(pack_kernel, halves),
        out_shape=[quarters] * 4,
        in_specs=[in_vmem],
        out_specs=[in_vmem] * 4,
        scratch_shapes=[VMEM((2, 4, rows, lanes), bf16)],
        cost_estimate=cost(COST_PACK),
        compiler_params=PARAMS,
    )(lam.transpose(0, 2, 1))
    far_mine = swap(to_mine, fetch, "lam_mine")
    far_other = swap(to_other, reduce, "lam_other")

    near_sibling = swap(sent_own, over_core, "sent_near_over_core")
    one_near = swap(jnp.stack([sent_own, near_sibling]), by_core(SENT), "sent_near_by_core")

    near, near_other = pl.pallas_call(
        split_kernel,
        out_shape=[half] * 2,
        in_specs=[in_vmem, in_vmem, pl.BlockSpec(memory_space=pl.ANY)],
        out_specs=[in_vmem] * 2,
        compiler_params=PARAMS,
    )(block_mask, integrals, to_mine)
    far = swap(near, fetch, "integrals_mine")
    near_other, one_near = lax.optimization_barrier((near_other, one_near))
    far_other_integrals = swap(near_other, reduce, "integrals_other")

    message = jax.ShapeDtypeStruct((4, rows, lanes), bf16)
    sent, sent_far, kept = pl.pallas_call(
        join_kernel,
        out_shape=[message, quarters, message],
        in_specs=[in_vmem] * 4,
        out_specs=[in_vmem] * 3,
        cost_estimate=cost(COST_JOIN),
        compiler_params=PARAMS,
    )(sent_own, kept_own, far_mine, far_other)

    def over_cores(array, scope):
        return swap(array, over_core, scope + "_over_core")

    def for_chip(own, sibling, hops, scope):
        return swap(jnp.stack([own, sibling]), by_core(hops), scope + "_by_core")

    def product(parts, kinds, hops, before=()):
        given = [(near, far), (near_other, far_other_integrals)]
        return pl.pallas_call(
            functools.partial(product_kernel, kinds, hops, bool(before), tuple(parts)),
            out_shape=[sums] * len(kinds),
            in_specs=[in_vmem] * (len(parts) + 2 * len(kinds) + len(before)),
            out_specs=[in_vmem] * len(kinds),
            cost_estimate=cost(0),
            compiler_params=PARAMS,
        )(*parts.values(), *(array for kind in kinds for array in given[kind]), *before)

    parts = dict(own=sent, sibling_near=near_sibling)
    parts["sibling_far"] = over_cores(sent_far, "sent_far")
    parts["alone"] = swap(sent, alone(SENT), "sent_alone")
    parts["one_far"] = for_chip(sent_far, parts["sibling_far"], SENT, "sent_far")
    kept_sibling = over_cores(kept, "kept")
    parts["alone"], kept_sibling = lax.optimization_barrier((parts["alone"], kept_sibling))
    kept_parts = dict(own=kept, sibling=kept_sibling)
    kept_parts["one"] = for_chip(kept, kept_sibling, KEPT, "kept")
    far = mark(COST_FAR, far)
    far_other_integrals = mark(COST_FAR_OTHER, far_other_integrals)
    parts["alone_sibling"] = over_cores(parts["alone"], "sent_alone")
    parts["one_far"], parts["alone_sibling"] = lax.optimization_barrier((parts["one_far"], parts["alone_sibling"]))
    parts["one_near"], parts["two_near"] = one_near, over_cores(one_near, "sent_near_one")
    last = dict(two_far=over_cores(parts["one_far"], "sent_far_one"))
    (sent,) = product(last, (0,), SENT, product(parts, (0,), SENT))
    (first_other,) = product(parts, (1,), SENT)
    kept, first_other = lax.optimization_barrier((kept, first_other))
    kept_parts["alone"] = swap(kept, alone(KEPT), "kept_alone")
    (sent_other,) = product(last, (1,), SENT, (first_other,))
    sum_mine = swap(sent, reduce, "sums_mine")
    sum_other = swap(sent_other, fetch, "sums_other")
    kept_parts, sent = lax.optimization_barrier((kept_parts, sent))
    kept_parts["two"] = over_cores(kept_parts["one"], "kept_one")
    kept_parts["alone_sibling"] = over_cores(kept_parts["alone"], "kept_alone")
    last = {name: kept_parts.pop(name) for name in ("alone", "alone_sibling")}
    kept, kept_other = product(last, (0, 1), KEPT, product(kept_parts, (0, 1), KEPT))
    return pl.pallas_call(
        total_kernel,
        out_shape=jax.ShapeDtypeStruct((irreps, rows, columns), bf16),
        in_specs=[in_vmem] * 4,
        out_specs=pl.BlockSpec(memory_space=pl.ANY),
        scratch_shapes=[VMEM((irreps, rows, columns), bf16), pltpu.SemaphoreType.DMA((irreps,))],
        compiler_params=PARAMS,
    )(kept, kept_other, sum_mine, sum_other)


def general(lam, integrals, block_mask):
    live = jnp.repeat(block_mask, lam.shape[2], axis=1) == 1
    kept = jnp.where(live[:, :, None], integrals, jnp.zeros_like(integrals))
    layer_lam = lax.all_gather(lam, "loop", axis=2, tiled=True)
    partial_sum = jnp.einsum("hpk,hka->hpa", layer_lam, kept, preferred_element_type=jnp.float32)
    return lax.psum_scatter(partial_sum, "rep", scatter_dimension=1, tiled=True).astype(jnp.bfloat16)


def solution(mesh):
    return jax.shard_map(
        square if (mesh.shape["rep"], mesh.shape["loop"]) == (4, 2 * CHIPS) else general,
        mesh=mesh,
        in_specs=(P(None, None, ("rep", "loop")), P(None, "rep", "loop"), P(None, "rep")),
        out_specs=P(None, "rep", "loop"),
        check_vma=False,
    )
```

```python
import functools

import jax
import jax.numpy as jnp
from jax import lax
from jax.experimental import pallas as pl
from jax.experimental.pallas import tpu as pltpu
from jax.sharding import PartitionSpec as P

VMEM = pltpu.VMEM
SENT, KEPT = (3, 1, 2), (1, 3, 2)
PARAMS = pltpu.CompilerParams(vmem_limit_bytes=16 << 20)
CHIPS = 4
COST_PACK, COST_JOIN, COST_FAR, COST_FAR_OTHER = 2 * 10**9, 4 * 10**9, 4 * 10**9, 2 * 10**9


def cost(flops):
    return pl.CostEstimate(flops=flops, bytes_accessed=0, transcendentals=0)


def swap(array, pairs, scope):
    with jax.named_scope(scope):
        return lax.ppermute(array, ("loop", "rep"), pairs)


def mark(flops, array):
    return pl.pallas_call(
        lambda *refs: None,
        out_shape=jax.ShapeDtypeStruct(array.shape, array.dtype),
        in_specs=[pl.BlockSpec(memory_space=VMEM)],
        out_specs=pl.BlockSpec(memory_space=VMEM),
        input_output_aliases={0: 0},
        cost_estimate=cost(flops),
        compiler_params=PARAMS,
    )(array)


def position():
    rep, spot = lax.axis_index("rep"), lax.axis_index("loop")
    return rep // 2, rep % 2, spot // 2, spot % 2


def pack_kernel(halves, lam_ref, sent_ref, kept_ref, to_mine_ref, to_other_ref, turned):
    y, x, _, core = position()
    rows = turned.shape[2]
    for kind in range(2):
        block = jnp.concatenate([lam_ref[kind * halves + h] for h in range(halves)], axis=0)
        flipped = block.T
        for quarter in range(4):
            turned[kind, quarter] = flipped[quarter * rows : (quarter + 1) * rows]
    kept, over_x, over_y, over_both = y * 2 + x, y * 2 + 1 - x, (1 - y) * 2 + x, (1 - y) * 2 + 1 - x
    for slot, (kind, to_ref) in enumerate(((core, to_mine_ref), (1 - core, to_other_ref))):
        summed, fetched = jnp.where(kind == 0, over_y, over_x), jnp.where(kind == 0, over_x, over_y)
        sent_ref[slot] = turned[kind, summed]
        kept_ref[slot] = turned[kind, kept]
        to_ref[0] = turned[kind, over_both]
        to_ref[1] = turned[kind, fetched]


def split_kernel(mask_ref, integrals_ref, _, mine_ref, other_ref):
    irreps, blocks = mask_ref.shape
    halves = irreps // 2
    _, depth, columns = integrals_ref.shape
    core = position()[3]
    for kind, out_ref in ((core, mine_ref), (1 - core, other_ref)):
        live = mask_ref[pl.ds(kind * halves, halves)].astype(jnp.float32)
        for h in range(halves):
            for b in range(blocks):
                rows = slice(b * depth // blocks, (b + 1) * depth // blocks)
                factor = jnp.broadcast_to(live[h : h + 1, b : b + 1], (depth // blocks, columns)).astype(jnp.bfloat16)
                out_ref[h, rows] = integrals_ref[kind * halves + h, rows] * factor


def join_kernel(sent_own_ref, kept_own_ref, far_mine_ref, far_other_ref, sent_ref, sent_far_ref, kept_ref):
    for which, (own_ref, out_ref) in enumerate(((sent_own_ref, sent_ref), (kept_own_ref, kept_ref))):
        for slot, ref in enumerate((far_mine_ref, far_other_ref)):
            out_ref[slot] = own_ref[slot]
            out_ref[2 + slot] = ref[which]
    sent_far_ref[0] = far_mine_ref[0]
    sent_far_ref[1] = far_other_ref[0]


def product_kernel(kinds, hops, held, names, *refs):
    count = len(names)
    messages, integrals_refs, rest = dict(zip(names, refs)), refs[count : count + 2 * len(kinds)], refs[count + 2 * len(kinds) :]
    before, out_refs = (rest[: len(kinds)], rest[len(kinds) :]) if held else (None, rest)
    _, _, z, core = position()
    by_core = jnp.where(core == 0, hops[1], hops[2])
    passed = jnp.where(core == 0, hops[2], hops[1])
    parts = []
    for name, ref in messages.items():
        layers = (0,) if "near" in name else (1,) if "far" in name else (0, 1)
        if "one" in name.split("_"):
            parts += [(ref.at[0], by_core, False, layers), (ref.at[1], by_core, True, layers)]
        elif "two" in name:
            parts += [(ref.at[0], passed, True, layers), (ref.at[1], passed, False, layers)]
        else:
            parts.append((ref, hops[0] if "alone" in name else 0, "sibling" in name, layers))
    for slot, kind in enumerate(kinds):
        integrals = integrals_refs[2 * slot : 2 * slot + 2]
        halves = integrals[0].shape[0]
        depth = messages[names[0]].shape[-1] // halves
        for h in range(halves):
            lam, kept = [], []
            for layer in range(2):
                for ref, hop, from_sibling, layers in parts:
                    if layer in layers:
                        block = (z ^ hop) * 2 + (1 - core if from_sibling else core)
                        unit = 2 * layers.index(layer) + (1 - kind if from_sibling else kind)
                        lam.append(ref[unit][:, h * depth : (h + 1) * depth])
                        kept.append(integrals[layer][h, pl.ds(pl.multiple_of(block * depth, depth), depth)])
            value = jnp.dot(
                jnp.concatenate(lam, axis=1), jnp.concatenate(kept, axis=0), preferred_element_type=jnp.float32
            )
            out_refs[slot][h] = before[slot][h] + value if held else value


def total_kernel(kept_ref, kept_other_ref, arrived_ref, arrived_other_ref, out_ref, rounded, done):
    core = position()[3]
    halves = kept_ref.shape[0]
    copies = []
    for kind, kept, arrived in ((0, kept_ref, arrived_ref), (1, kept_other_ref, arrived_other_ref)):
        at = (1 - core if kind else core) * halves
        for h in range(halves):
            step = kind * halves + h
            rounded[step] = (kept[h] + arrived[h]).astype(rounded.dtype)
            copies.append(pltpu.make_async_copy(rounded.at[step], out_ref.at[at + h], done.at[step]))
            copies[-1].start()
    for copy in copies:
        copy.wait()


def square(lam, integrals, block_mask):
    irreps, occ, depth = lam.shape
    halves = irreps // 2
    rows = occ // 4
    columns = integrals.shape[2]
    loops = 2 * CHIPS
    bf16, f32 = jnp.bfloat16, jnp.float32
    lanes = halves * depth
    in_vmem = pl.BlockSpec(memory_space=VMEM)
    quarters = jax.ShapeDtypeStruct((2, rows, lanes), bf16)
    half = jax.ShapeDtypeStruct((halves,) + integrals.shape[1:], bf16)
    sums = jax.ShapeDtypeStruct((halves, rows, columns), f32)

    def pairs(aim):
        places = [(s, r) for s in range(loops) for r in range(4)]
        return [(at, places.index(aim(s, r, s % 2))) for at, (s, r) in enumerate(places)]

    over_core = pairs(lambda s, r, core: (s ^ 1, r))
    fetch = pairs(lambda s, r, core: (s, r ^ (1 + core)))
    reduce = pairs(lambda s, r, core: (s, r ^ (2 - core)))
    alone = lambda hops: pairs(lambda s, r, core: (s ^ (2 * hops[0]), r))
    by_core = lambda hops: pairs(lambda s, r, core: (s ^ (2 * hops[1 + core]), r))

    sent_own, kept_own, to_mine, to_other = pl.pallas_call(
        functools.partial(pack_kernel, halves),
        out_shape=[quarters] * 4,
        in_specs=[in_vmem],
        out_specs=[in_vmem] * 4,
        scratch_shapes=[VMEM((2, 4, rows, lanes), bf16)],
        cost_estimate=cost(COST_PACK),
        compiler_params=PARAMS,
    )(lam.transpose(0, 2, 1))
    far_mine = swap(to_mine, fetch, "lam_mine")
    far_other = swap(to_other, reduce, "lam_other")

    near_sibling = swap(sent_own, over_core, "sent_near_over_core")
    one_near = swap(jnp.stack([sent_own, near_sibling]), by_core(SENT), "sent_near_by_core")

    near, near_other = pl.pallas_call(
        split_kernel,
        out_shape=[half] * 2,
        in_specs=[in_vmem, in_vmem, pl.BlockSpec(memory_space=pl.ANY)],
        out_specs=[in_vmem] * 2,
        compiler_params=PARAMS,
    )(block_mask, integrals, to_mine)
    far = swap(near, fetch, "integrals_mine")
    near_other, one_near = lax.optimization_barrier((near_other, one_near))
    far_other_integrals = swap(near_other, reduce, "integrals_other")

    message = jax.ShapeDtypeStruct((4, rows, lanes), bf16)
    sent, sent_far, kept = pl.pallas_call(
        join_kernel,
        out_shape=[message, quarters, message],
        in_specs=[in_vmem] * 4,
        out_specs=[in_vmem] * 3,
        cost_estimate=cost(COST_JOIN),
        compiler_params=PARAMS,
    )(sent_own, kept_own, far_mine, far_other)

    def over_cores(array, scope):
        return swap(array, over_core, scope + "_over_core")

    def for_chip(own, sibling, hops, scope):
        return swap(jnp.stack([own, sibling]), by_core(hops), scope + "_by_core")

    def product(parts, kinds, hops, before=()):
        given = [(near, far), (near_other, far_other_integrals)]
        return pl.pallas_call(
            functools.partial(product_kernel, kinds, hops, bool(before), tuple(parts)),
            out_shape=[sums] * len(kinds),
            in_specs=[in_vmem] * (len(parts) + 2 * len(kinds) + len(before)),
            out_specs=[in_vmem] * len(kinds),
            cost_estimate=cost(0),
            compiler_params=PARAMS,
        )(*parts.values(), *(array for kind in kinds for array in given[kind]), *before)

    parts = dict(own=sent, sibling_near=near_sibling)
    parts["sibling_far"] = over_cores(sent_far, "sent_far")
    parts["alone"] = swap(sent, alone(SENT), "sent_alone")
    parts["one_far"] = for_chip(sent_far, parts["sibling_far"], SENT, "sent_far")
    kept_sibling = over_cores(kept, "kept")
    parts["alone"], kept_sibling = lax.optimization_barrier((parts["alone"], kept_sibling))
    kept_parts = dict(own=kept, sibling=kept_sibling)
    kept_parts["one"] = for_chip(kept, kept_sibling, KEPT, "kept")
    far = mark(COST_FAR, far)
    far_other_integrals = mark(COST_FAR_OTHER, far_other_integrals)
    parts["alone_sibling"] = over_cores(parts["alone"], "sent_alone")
    parts["one_far"], parts["alone_sibling"] = lax.optimization_barrier((parts["one_far"], parts["alone_sibling"]))
    parts["one_near"], parts["two_near"] = one_near, over_cores(one_near, "sent_near_one")
    last = dict(two_far=over_cores(parts["one_far"], "sent_far_one"))
    (sent,) = product(last, (0,), SENT, product(parts, (0,), SENT))
    (first_other,) = product(parts, (1,), SENT)
    kept, first_other = lax.optimization_barrier((kept, first_other))
    kept_parts["alone"] = swap(kept, alone(KEPT), "kept_alone")
    (sent_other,) = product(last, (1,), SENT, (first_other,))
    sum_mine = swap(sent, reduce, "sums_mine")
    sum_other = swap(sent_other, fetch, "sums_other")
    kept_parts, sent = lax.optimization_barrier((kept_parts, sent))
    kept_parts["two"] = over_cores(kept_parts["one"], "kept_one")
    kept_parts["alone_sibling"] = over_cores(kept_parts["alone"], "kept_alone")
    last = {name: kept_parts.pop(name) for name in ("two", "alone_sibling")}
    kept, kept_other = product(last, (0, 1), KEPT, product(kept_parts, (0, 1), KEPT))
    return pl.pallas_call(
        total_kernel,
        out_shape=jax.ShapeDtypeStruct((irreps, rows, columns), bf16),
        in_specs=[in_vmem] * 4,
        out_specs=pl.BlockSpec(memory_space=pl.ANY),
        scratch_shapes=[VMEM((irreps, rows, columns), bf16), pltpu.SemaphoreType.DMA((irreps,))],
        compiler_params=PARAMS,
    )(kept, kept_other, sum_mine, sum_other)


def general(lam, integrals, block_mask):
    live = jnp.repeat(block_mask, lam.shape[2], axis=1) == 1
    kept = jnp.where(live[:, :, None], integrals, jnp.zeros_like(integrals))
    layer_lam = lax.all_gather(lam, "loop", axis=2, tiled=True)
    partial_sum = jnp.einsum("hpk,hka->hpa", layer_lam, kept, preferred_element_type=jnp.float32)
    return lax.psum_scatter(partial_sum, "rep", scatter_dimension=1, tiled=True).astype(jnp.bfloat16)


def solution(mesh):
    return jax.shard_map(
        square if (mesh.shape["rep"], mesh.shape["loop"]) == (4, 2 * CHIPS) else general,
        mesh=mesh,
        in_specs=(P(None, None, ("rep", "loop")), P(None, "rep", "loop"), P(None, "rep")),
        out_specs=P(None, "rep", "loop"),
        check_vma=False,
    )
```

```python
import functools

import jax
import jax.numpy as jnp
from jax import lax
from jax.experimental import pallas as pl
from jax.experimental.pallas import tpu as pltpu
from jax.sharding import PartitionSpec as P

VMEM = pltpu.VMEM
SENT, KEPT = (3, 1, 2), (1, 3, 2)
PARAMS = pltpu.CompilerParams(vmem_limit_bytes=16 << 20)
CHIPS = 4
COST_PACK, COST_JOIN, COST_FAR, COST_FAR_OTHER = 2 * 10**9, 4 * 10**9, 4 * 10**9, 2 * 10**9


def cost(flops):
    return pl.CostEstimate(flops=flops, bytes_accessed=0, transcendentals=0)


def swap(array, pairs, scope):
    with jax.named_scope(scope):
        return lax.ppermute(array, ("loop", "rep"), pairs)


def mark(flops, array):
    return pl.pallas_call(
        lambda *refs: None,
        out_shape=jax.ShapeDtypeStruct(array.shape, array.dtype),
        in_specs=[pl.BlockSpec(memory_space=VMEM)],
        out_specs=pl.BlockSpec(memory_space=VMEM),
        input_output_aliases={0: 0},
        cost_estimate=cost(flops),
        compiler_params=PARAMS,
    )(array)


def position():
    rep, spot = lax.axis_index("rep"), lax.axis_index("loop")
    return rep // 2, rep % 2, spot // 2, spot % 2


def pack_kernel(halves, lam_ref, sent_ref, kept_ref, to_mine_ref, to_other_ref, turned):
    y, x, _, core = position()
    rows = turned.shape[2]
    for kind in range(2):
        block = jnp.concatenate([lam_ref[kind * halves + h] for h in range(halves)], axis=0)
        flipped = block.T
        for quarter in range(4):
            turned[kind, quarter] = flipped[quarter * rows : (quarter + 1) * rows]
    kept, over_x, over_y, over_both = y * 2 + x, y * 2 + 1 - x, (1 - y) * 2 + x, (1 - y) * 2 + 1 - x
    for slot, (kind, to_ref) in enumerate(((core, to_mine_ref), (1 - core, to_other_ref))):
        summed, fetched = jnp.where(kind == 0, over_y, over_x), jnp.where(kind == 0, over_x, over_y)
        sent_ref[slot] = turned[kind, summed]
        kept_ref[slot] = turned[kind, kept]
        to_ref[0] = turned[kind, over_both]
        to_ref[1] = turned[kind, fetched]


def split_kernel(mask_ref, integrals_ref, _, mine_ref, other_ref):
    irreps, blocks = mask_ref.shape
    halves = irreps // 2
    _, depth, columns = integrals_ref.shape
    core = position()[3]
    for kind, out_ref in ((core, mine_ref), (1 - core, other_ref)):
        live = mask_ref[pl.ds(kind * halves, halves)].astype(jnp.float32)
        for h in range(halves):
            for b in range(blocks):
                rows = slice(b * depth // blocks, (b + 1) * depth // blocks)
                factor = jnp.broadcast_to(live[h : h + 1, b : b + 1], (depth // blocks, columns)).astype(jnp.bfloat16)
                out_ref[h, rows] = integrals_ref[kind * halves + h, rows] * factor


def join_kernel(sent_own_ref, kept_own_ref, far_mine_ref, far_other_ref, sent_ref, sent_far_ref, kept_ref):
    for which, (own_ref, out_ref) in enumerate(((sent_own_ref, sent_ref), (kept_own_ref, kept_ref))):
        for slot, ref in enumerate((far_mine_ref, far_other_ref)):
            out_ref[slot] = own_ref[slot]
            out_ref[2 + slot] = ref[which]
    sent_far_ref[0] = far_mine_ref[0]
    sent_far_ref[1] = far_other_ref[0]


def product_kernel(kinds, hops, held, names, *refs):
    count = len(names)
    messages, integrals_refs, rest = dict(zip(names, refs)), refs[count : count + 2 * len(kinds)], refs[count + 2 * len(kinds) :]
    before, out_refs = (rest[: len(kinds)], rest[len(kinds) :]) if held else (None, rest)
    _, _, z, core = position()
    by_core = jnp.where(core == 0, hops[1], hops[2])
    passed = jnp.where(core == 0, hops[2], hops[1])
    parts = []
    for name, ref in messages.items():
        layers = (0,) if "near" in name else (1,) if "far" in name else (0, 1)
        if "one" in name.split("_"):
            parts += [(ref.at[0], by_core, False, layers), (ref.at[1], by_core, True, layers)]
        elif "two" in name:
            parts += [(ref.at[0], passed, True, layers), (ref.at[1], passed, False, layers)]
        else:
            parts.append((ref, hops[0] if "alone" in name else 0, "sibling" in name, layers))
    for slot, kind in enumerate(kinds):
        integrals = integrals_refs[2 * slot : 2 * slot + 2]
        halves = integrals[0].shape[0]
        depth = messages[names[0]].shape[-1] // halves
        for h in range(halves):
            lam, kept = [], []
            for layer in range(2):
                for ref, hop, from_sibling, layers in parts:
                    if layer in layers:
                        block = (z ^ hop) * 2 + (1 - core if from_sibling else core)
                        unit = 2 * layers.index(layer) + (1 - kind if from_sibling else kind)
                        lam.append(ref[unit][:, h * depth : (h + 1) * depth])
                        kept.append(integrals[layer][h, pl.ds(pl.multiple_of(block * depth, depth), depth)])
            value = jnp.dot(
                jnp.concatenate(lam, axis=1), jnp.concatenate(kept, axis=0), preferred_element_type=jnp.float32
            )
            out_refs[slot][h] = before[slot][h] + value if held else value


def total_kernel(kept_ref, kept_other_ref, arrived_ref, arrived_other_ref, out_ref, rounded, done):
    core = position()[3]
    halves = kept_ref.shape[0]
    copies = []
    for kind, kept, arrived in ((0, kept_ref, arrived_ref), (1, kept_other_ref, arrived_other_ref)):
        at = (1 - core if kind else core) * halves
        rounded[kind] = (kept[...] + arrived[...]).astype(rounded.dtype)
        copies.append(pltpu.make_async_copy(rounded.at[kind], out_ref.at[pl.ds(at, halves)], done.at[kind]))
        copies[-1].start()
    for copy in copies:
        copy.wait()


def square(lam, integrals, block_mask):
    irreps, occ, depth = lam.shape
    halves = irreps // 2
    rows = occ // 4
    columns = integrals.shape[2]
    loops = 2 * CHIPS
    bf16, f32 = jnp.bfloat16, jnp.float32
    lanes = halves * depth
    in_vmem = pl.BlockSpec(memory_space=VMEM)
    quarters = jax.ShapeDtypeStruct((2, rows, lanes), bf16)
    half = jax.ShapeDtypeStruct((halves,) + integrals.shape[1:], bf16)
    sums = jax.ShapeDtypeStruct((halves, rows, columns), f32)

    def pairs(aim):
        places = [(s, r) for s in range(loops) for r in range(4)]
        return [(at, places.index(aim(s, r, s % 2))) for at, (s, r) in enumerate(places)]

    over_core = pairs(lambda s, r, core: (s ^ 1, r))
    fetch = pairs(lambda s, r, core: (s, r ^ (1 + core)))
    reduce = pairs(lambda s, r, core: (s, r ^ (2 - core)))
    alone = lambda hops: pairs(lambda s, r, core: (s ^ (2 * hops[0]), r))
    by_core = lambda hops: pairs(lambda s, r, core: (s ^ (2 * hops[1 + core]), r))

    sent_own, kept_own, to_mine, to_other = pl.pallas_call(
        functools.partial(pack_kernel, halves),
        out_shape=[quarters] * 4,
        in_specs=[in_vmem],
        out_specs=[in_vmem] * 4,
        scratch_shapes=[VMEM((2, 4, rows, lanes), bf16)],
        cost_estimate=cost(COST_PACK),
        compiler_params=PARAMS,
    )(lam.transpose(0, 2, 1))
    far_mine = swap(to_mine, fetch, "lam_mine")
    far_other = swap(to_other, reduce, "lam_other")

    near_sibling = swap(sent_own, over_core, "sent_near_over_core")
    one_near = swap(jnp.stack([sent_own, near_sibling]), by_core(SENT), "sent_near_by_core")

    near, near_other = pl.pallas_call(
        split_kernel,
        out_shape=[half] * 2,
        in_specs=[in_vmem, in_vmem, pl.BlockSpec(memory_space=pl.ANY)],
        out_specs=[in_vmem] * 2,
        compiler_params=PARAMS,
    )(block_mask, integrals, to_mine)
    far = swap(near, fetch, "integrals_mine")
    near_other, one_near = lax.optimization_barrier((near_other, one_near))
    far_other_integrals = swap(near_other, reduce, "integrals_other")

    message = jax.ShapeDtypeStruct((4, rows, lanes), bf16)
    sent, sent_far, kept = pl.pallas_call(
        join_kernel,
        out_shape=[message, quarters, message],
        in_specs=[in_vmem] * 4,
        out_specs=[in_vmem] * 3,
        cost_estimate=cost(COST_JOIN),
        compiler_params=PARAMS,
    )(sent_own, kept_own, far_mine, far_other)

    def over_cores(array, scope):
        return swap(array, over_core, scope + "_over_core")

    def for_chip(own, sibling, hops, scope):
        return swap(jnp.stack([own, sibling]), by_core(hops), scope + "_by_core")

    def product(parts, kinds, hops, before=()):
        given = [(near, far), (near_other, far_other_integrals)]
        return pl.pallas_call(
            functools.partial(product_kernel, kinds, hops, bool(before), tuple(parts)),
            out_shape=[sums] * len(kinds),
            in_specs=[in_vmem] * (len(parts) + 2 * len(kinds) + len(before)),
            out_specs=[in_vmem] * len(kinds),
            cost_estimate=cost(0),
            compiler_params=PARAMS,
        )(*parts.values(), *(array for kind in kinds for array in given[kind]), *before)

    parts = dict(own=sent, sibling_near=near_sibling)
    parts["sibling_far"] = over_cores(sent_far, "sent_far")
    parts["alone"] = swap(sent, alone(SENT), "sent_alone")
    parts["one_far"] = for_chip(sent_far, parts["sibling_far"], SENT, "sent_far")
    kept_sibling = over_cores(kept, "kept")
    parts["alone"], kept_sibling = lax.optimization_barrier((parts["alone"], kept_sibling))
    kept_parts = dict(own=kept, sibling=kept_sibling)
    kept_parts["one"] = for_chip(kept, kept_sibling, KEPT, "kept")
    far = mark(COST_FAR, far)
    far_other_integrals = mark(COST_FAR_OTHER, far_other_integrals)
    parts["alone_sibling"] = over_cores(parts["alone"], "sent_alone")
    parts["one_far"], parts["alone_sibling"] = lax.optimization_barrier((parts["one_far"], parts["alone_sibling"]))
    parts["one_near"], parts["two_near"] = one_near, over_cores(one_near, "sent_near_one")
    last = dict(two_far=over_cores(parts["one_far"], "sent_far_one"))
    (sent,) = product(last, (0,), SENT, product(parts, (0,), SENT))
    (first_other,) = product(parts, (1,), SENT)
    kept, first_other = lax.optimization_barrier((kept, first_other))
    kept_parts["alone"] = swap(kept, alone(KEPT), "kept_alone")
    (sent_other,) = product(last, (1,), SENT, (first_other,))
    sum_mine = swap(sent, reduce, "sums_mine")
    sum_other = swap(sent_other, fetch, "sums_other")
    kept_parts, sent = lax.optimization_barrier((kept_parts, sent))
    kept_parts["two"] = over_cores(kept_parts["one"], "kept_one")
    kept_parts["alone_sibling"] = over_cores(kept_parts["alone"], "kept_alone")
    last = {name: kept_parts.pop(name) for name in ("two", "alone_sibling")}
    kept, kept_other = product(last, (0, 1), KEPT, product(kept_parts, (0, 1), KEPT))
    return pl.pallas_call(
        total_kernel,
        out_shape=jax.ShapeDtypeStruct((irreps, rows, columns), bf16),
        in_specs=[in_vmem] * 4,
        out_specs=pl.BlockSpec(memory_space=pl.ANY),
        scratch_shapes=[VMEM((2,) + sums.shape, bf16), pltpu.SemaphoreType.DMA((2,))],
        compiler_params=PARAMS,
    )(kept, kept_other, sum_mine, sum_other)


def general(lam, integrals, block_mask):
    live = jnp.repeat(block_mask, lam.shape[2], axis=1) == 1
    kept = jnp.where(live[:, :, None], integrals, jnp.zeros_like(integrals))
    layer_lam = lax.all_gather(lam, "loop", axis=2, tiled=True)
    partial_sum = jnp.einsum("hpk,hka->hpa", layer_lam, kept, preferred_element_type=jnp.float32)
    return lax.psum_scatter(partial_sum, "rep", scatter_dimension=1, tiled=True).astype(jnp.bfloat16)


def solution(mesh):
    return jax.shard_map(
        square if (mesh.shape["rep"], mesh.shape["loop"]) == (4, 2 * CHIPS) else general,
        mesh=mesh,
        in_specs=(P(None, None, ("rep", "loop")), P(None, "rep", "loop"), P(None, "rep")),
        out_specs=P(None, "rep", "loop"),
        check_vma=False,
    )
```
